32 devices in a mesh: layer: 2 (over core), rows: 16 (over z, y, x).
Axes of the slice: x: 2, y: 2, z: 4, core: 2. Of those that a mesh axis runs over, the one named last changes fastest.
Arguments:
- frames: bfloat16 [3, 4, 32, 64, 128], P(None, None, 'rows'), may hold values from -6 to 6
- hidden_in: bfloat16 [4, 4, 32, 64, 128], P('layer', None, 'rows'), may hold values from -4 to 4
- cell_in: bfloat16 [4, 4, 32, 64, 128], P('layer', None, 'rows'), may hold values from -6 to 6
- memory_in: bfloat16 [4, 32, 64, 128], P(None, 'rows'), may hold values from -6 to 6
- w_x: bfloat16 [4, 576, 448], P('layer'), may hold values from -0.25 to 0.25
- w_h: bfloat16 [4, 576, 256], P('layer'), may hold values from -0.25 to 0.25
- w_m: bfloat16 [4, 576, 192], P('layer'), may hold values from -0.25 to 0.25
- w_o: bfloat16 [4, 1152, 64], P('layer'), may hold values from -0.1875 to 0.1875
- w_last: bfloat16 [4, 128, 64], P('layer'), may hold values from -0.5 to 0.5
Outputs:
- hidden_out: bfloat16 [4, 4, 32, 64, 128], P('layer', None, 'rows')
- cell_out: bfloat16 [4, 4, 32, 64, 128], P('layer', None, 'rows')
- memory_out: bfloat16 [2, 4, 32, 64, 128], P('layer', None, 'rows')
The draws below stay inside these ranges and needn't reach their ends.
All inputs are finite; a program needn't handle non-finite values.
Results may differ from the reference program's by a relative error of at most 0.014.
Values may be sent and summed in bfloat16 or wider, within the bound.
A program may use at most 64 MiB of HBM per device.

```python
import jax
import jax.numpy as jnp
from jax import lax

CH = 64
GW = 128
SEQS = 4
STEPS = 3
LAYERS = 4
GH = 32


def level_of(rng, shape, cuts, low, top_value):
    def one(position, parts):
        steps = jax.random.uniform(jax.random.fold_in(jax.random.fold_in(rng, 6), position), (parts,), jnp.float32, low / len(cuts), top_value / len(cuts))
        return jnp.repeat(jnp.exp(steps), shape[position] // parts).reshape((-1,) + (1,) * (len(shape) - position - 1))

    factor_of = one(*cuts[0])
    for cut in cuts[1:]:
        factor_of = factor_of * one(*cut)
    return factor_of


def centred(key, extent, spread, reach, cuts=(), kind=jnp.bfloat16):
    result = spread * jax.random.normal(key, extent, jnp.float32)
    if cuts:
        result = result * level_of(key, extent, cuts, -0.22, 0.18)
    return jnp.clip(result, -reach, reach).astype(kind)


def setup_inputs(seed: int = 0) -> dict:
    key_list = jax.random.split(jax.random.key(seed), 10)
    return {
        "frames": centred(key_list[0], (STEPS, SEQS, GH, CH, GW), 1.0, 6.0, ((2, 16),)),
        "hidden_in": centred(key_list[1], (LAYERS, SEQS, GH, CH, GW), 0.7, 4.0, ((0, 2), (2, 16))),
        "cell_in": centred(key_list[2], (LAYERS, SEQS, GH, CH, GW), 1.0, 6.0, ((0, 2), (2, 16))),
        "memory_in": centred(key_list[3], (SEQS, GH, CH, GW), 1.0, 6.0, ((1, 16),)),
        "w_x": centred(key_list[4], (LAYERS, 9 * CH, 7 * CH), (9 * CH) ** -0.5, 0.25, ((0, 2),)),
        "w_h": centred(key_list[5], (LAYERS, 9 * CH, 4 * CH), (9 * CH) ** -0.5, 0.25, ((0, 2),)),
        "w_m": centred(key_list[6], (LAYERS, 9 * CH, 3 * CH), (9 * CH) ** -0.5, 0.25, ((0, 2),)),
        "w_o": centred(key_list[7], (LAYERS, 18 * CH, CH), (18 * CH) ** -0.5, 0.1875, ((0, 2),)),
        "w_last": centred(key_list[8], (LAYERS, 2 * CH, CH), (2 * CH) ** -0.5, 0.5, ((0, 2),)),
    }


def shifted_taps(padded, height):
    pieces = []
    for row_offset in range(3):
        row_band = padded[:, row_offset:row_offset + height]
        zero_column = jnp.zeros_like(row_band[..., :1])
        pieces.append(jnp.concatenate([zero_column, row_band[..., :-1]], axis=-1))
        pieces.append(row_band)
        pieces.append(jnp.concatenate([row_band[..., 1:], zero_column], axis=-1))
    return jnp.concatenate(pieces, axis=2)


def convolve(padded, weight, height):
    taps = shifted_taps(padded, height).astype(jnp.float32)
    return jnp.einsum("ko,brkw->brow", weight.astype(jnp.float32), taps, precision=lax.Precision.HIGHEST)


def gate_math(input_gates, hidden_gates, memory_gates, cell_prev, memory_prev):
    parts_x = jnp.split(input_gates, 7, axis=2)
    parts_h = jnp.split(hidden_gates, 4, axis=2)
    parts_m = jnp.split(memory_gates, 3, axis=2)
    cell_new = (jax.nn.sigmoid(parts_x[1] + parts_h[1] + 1.0) * cell_prev.astype(jnp.float32)
                + jax.nn.sigmoid(parts_x[0] + parts_h[0]) * jnp.tanh(parts_x[2] + parts_h[2])).astype(jnp.bfloat16)
    memory_new = (jax.nn.sigmoid(parts_x[4] + parts_m[1] + 1.0) * memory_prev.astype(jnp.float32)
                  + jax.nn.sigmoid(parts_x[3] + parts_m[0]) * jnp.tanh(parts_x[5] + parts_m[2])).astype(jnp.bfloat16)
    return cell_new, memory_new, parts_x[6] + parts_h[3]


def pad_rows(field):
    return jnp.pad(field, ((0, 0), (1, 1), (0, 0), (0, 0)))


def reference_cell(layer_input, hidden_prev, cell_prev, memory_prev, weight_x, weight_h, weight_m, weight_o, weight_last):
    height = layer_input.shape[1]
    input_gates = convolve(pad_rows(layer_input), weight_x, height)
    hidden_gates = convolve(pad_rows(hidden_prev), weight_h, height)
    memory_gates = convolve(pad_rows(memory_prev), weight_m, height)
    cell_new, memory_new, output_part = gate_math(input_gates, hidden_gates, memory_gates, cell_prev, memory_prev)
    memory_pair = jnp.concatenate([cell_new, memory_new], axis=2)
    output_gate = jax.nn.sigmoid(output_part + convolve(pad_rows(memory_pair), weight_o, height))
    mixed = jnp.einsum("ko,brkw->brow", weight_last.astype(jnp.float32), memory_pair.astype(jnp.float32), precision=lax.Precision.HIGHEST)
    hidden_new = (output_gate * jnp.tanh(mixed)).astype(jnp.bfloat16)
    return hidden_new, cell_new, memory_new


def reference(frames, hidden_in, cell_in, memory_in, w_x, w_h, w_m, w_o, w_last):
    hidden_list = [hidden_in[layer_index] for layer_index in range(LAYERS)]
    cell_list = [cell_in[layer_index] for layer_index in range(LAYERS)]
    memory_now = memory_in
    top_list = []
    for time_index in range(STEPS):
        layer_input = frames[time_index]
        for layer_index in range(LAYERS):
            hidden_new, cell_new, memory_now = reference_cell(
                layer_input, hidden_list[layer_index], cell_list[layer_index], memory_now,
                w_x[layer_index], w_h[layer_index], w_m[layer_index], w_o[layer_index], w_last[layer_index])
            hidden_list[layer_index] = hidden_new
            cell_list[layer_index] = cell_new
            layer_input = hidden_new
            if time_index == STEPS - 1 and layer_index % 2 == 1:
                top_list.append(memory_now)
    return jnp.stack(hidden_list), jnp.stack(cell_list), jnp.stack(top_list)
```

```python
import functools

import jax
import jax.numpy as jnp
from jax import lax
from jax.experimental import pallas as pl
from jax.experimental.pallas import tpu as pltpu
from jax.sharding import PartitionSpec as P

MESH = pl.DeviceIdType.MESH
F32 = jnp.float32
BF16 = jnp.bfloat16


def sig(x):
    return 0.5 * jnp.tanh(0.5 * x) + 0.5


def kernel(
    rows_total, layers, steps,
    frames, hidden, cell, memory, weights,
    hid_out, cell_out, mem_out,
    taps, wbuf, land_h, land_c, land_cs, land_m, land_f,
    h_send, h_land, m_send, m_land, cell_state, mem_state, cell_last, acc_h, acc_m, acc_o,
    r_w, s_w, r_h, s_h, s_hc, r_c, r_cs, s_c, s_cc, r_m, s_m, r_f, s_f,
    r_hl, s_hl, r_ml, s_ml, r_out, s_out, l_out,
):
    core, row = lax.axis_index("layer"), lax.axis_index("rows")
    other = 1 - core
    local_layers, seqs_all, band, ch, width = hidden.shape
    cores = layers // local_layers
    seqs = seqs_all // cores
    cells = layers * steps
    tap = 3 * ch
    span = band + 4
    t_frame, t_mem, t_cell = 0, layers + 1, layers + 2
    has_up, has_down = row > 0, row < rows_total - 1
    up, down = lax.rem(row + rows_total - 1, rows_total), lax.rem(row + 1, rows_total)

    def to(c, r):
        return {"layer": c, "rows": r}

    def remote(src, dst, send, recv, c, r):
        return pltpu.make_async_remote_copy(
            src_ref=src, dst_ref=dst, send_sem=send, recv_sem=recv,
            device_id=to(c, r), device_id_type=MESH,
        )

    def arrived(dst, sem):
        pltpu.make_async_copy(dst, dst, sem).wait()

    lane = lax.broadcasted_iota(jnp.int32, (ch, width), 1)

    def put_taps(index, r, s, value):
        wide = value.astype(F32)
        left = jnp.where(lane == 0, 0.0, pltpu.roll(wide, 1, 1)).astype(BF16)
        right = jnp.where(lane == width - 1, 0.0, pltpu.roll(wide, width - 1, 1)).astype(BF16)
        cols = slice(s * width, (s + 1) * width)
        taps[index, r * tap : r * tap + ch, cols] = left
        taps[index, r * tap + ch : r * tap + 2 * ch, cols] = value.astype(BF16)
        taps[index, r * tap + 2 * ch : (r + 1) * tap, cols] = right

    def window(index, r):
        return taps[index, (r - 1) * tap : (r + 2) * tap, :]

    barrier = pltpu.get_barrier_semaphore()
    pl.semaphore_signal(barrier, inc=1, device_id=to(other, row), device_id_type=MESH)

    @pl.when(has_up)
    def _():
        for c in range(cores):
            pl.semaphore_signal(barrier, inc=1, device_id=to(c, up), device_id_type=MESH)

    @pl.when(has_down)
    def _():
        for c in range(cores):
            pl.semaphore_signal(barrier, inc=1, device_id=to(c, down), device_id_type=MESH)

    edge = 2 * tap
    for index in range(layers + 3):
        taps[index, :edge, :] = jnp.zeros((edge, taps.shape[2]), BF16)
        taps[index, (span - 2) * tap :, :] = jnp.zeros((edge, taps.shape[2]), BF16)
    mem_state[0] = jnp.zeros(mem_state.shape[1:], BF16)
    mem_state[band + 1] = jnp.zeros(mem_state.shape[1:], BF16)
    for layer in range(layers):
        cell_state[layer, 0] = jnp.zeros(mem_state.shape[1:], BF16)
        cell_state[layer, band + 1] = jnp.zeros(mem_state.shape[1:], BF16)

    near = has_up.astype(jnp.int32) + has_down.astype(jnp.int32)
    pl.semaphore_wait(barrier, 1 + cores * near)

    mine = pl.ds(core * seqs, seqs)
    theirs = pl.ds(other * seqs, seqs)

    def center_copies(j):
        layer = core * local_layers + j
        local = [
            pltpu.make_async_copy(weights.at[j], wbuf.at[layer], r_w.at[layer]),
            pltpu.make_async_copy(hidden.at[j, mine], land_h.at[layer, 1], r_h.at[layer, 1]),
            pltpu.make_async_copy(cell.at[j, mine], land_c.at[layer], r_c.at[layer]),
        ]
        far = [
            remote(weights.at[j], wbuf.at[layer], s_w.at[j], r_w.at[layer], other, row),
            remote(hidden.at[j, theirs], land_h.at[layer, 1], s_hc.at[j], r_h.at[layer, 1], other, row),
            remote(cell.at[j, theirs], land_c.at[layer], s_cc.at[j], r_c.at[layer], other, row),
        ]
        return local, far

    def halo_copies(j, side):
        layer = core * local_layers + j
        target = down if side == 0 else up
        edge_row = band - 1 if side == 0 else 0
        result = []
        for c in range(cores):
            part = pl.ds(c * seqs, seqs)
            result.append(remote(hidden.at[j, part], land_h.at[layer, 2 * side],
                                 s_h.at[j, c, side], r_h.at[layer, 2 * side], c, target))
            result.append(remote(cell.at[j, part, edge_row], land_cs.at[layer, side],
                                 s_c.at[j, c, side], r_cs.at[layer, side], c, target))
        return result

    def frame_copy(t, side):
        target = down if side == 0 else up
        return remote(frames.at[t, mine], land_f.at[t, side], s_f.at[t, side], r_f.at[t, side], core, target)

    def memory_copy(side):
        target = down if side == 0 else up
        return remote(memory.at[mine], land_m.at[side], s_m.at[side], r_m.at[side], core, target)

    sides = ((0, has_down), (1, has_up))
    from_sides = ((0, has_up), (1, has_down))

    for j in range(local_layers):
        local, far = center_copies(j)
        for copy in far + local:
            copy.start()
        for side, there in sides:

            @pl.when(there)
            def _():
                if j == 0:
                    memory_copy(side).start()
                    frame_copy(0, side).start()
                for copy in halo_copies(j, side):
                    copy.start()

    for t in range(1, steps):
        for side, there in sides:

            @pl.when(there)
            def _():
                frame_copy(t, side).start()

    for s in range(seqs):
        cols = slice(s * width, (s + 1) * width)
        for r in range(band):
            value = memory[core * seqs + s, r]
            put_taps(t_mem, 2 + r, s, value)
            mem_state[1 + r, :, cols] = value
    for side, there in from_sides:

        @pl.when(there)
        def _():
            arrived(land_m.at[side], r_m.at[side])
            first = 0 if side == 0 else span - 2
            for s in range(seqs):
                cols = slice(s * width, (s + 1) * width)
                for r in range(2):
                    put_taps(t_mem, first + r, s, land_m[side, s, r])
                if side == 0:
                    mem_state[0, :, cols] = land_m[side, s, band - 1]
                else:
                    mem_state[band + 1, :, cols] = land_m[side, s, 0]

    def h_copy(k, side):
        target = down if side == 0 else up
        return remote(h_send.at[k], h_land.at[k, side], s_hl.at[k, side], r_hl.at[k, side], core, target)

    def m_copy(k, side):
        target = down if side == 0 else up
        edge_row = 0 if side == 0 else band - 1
        return remote(m_send.at[k, :, edge_row], m_land.at[k, side], s_ml.at[k, side], r_ml.at[k, side], core, target)

    def step(k, carry):
        layer = lax.rem(k, layers)
        t = lax.div(k, layers)
        prev = lax.rem(k + cells - 1, cells)
        before = lax.rem(k + layers - 1, layers)

        @pl.when(k < layers)
        def _():
            arrived(wbuf.at[layer], r_w.at[layer])
            arrived(land_h.at[layer, 1], r_h.at[layer, 1])
            arrived(land_c.at[layer], r_c.at[layer])
            for s in range(seqs):
                cols = slice(s * width, (s + 1) * width)
                for r in range(band):
                    put_taps(layer + 1, 2 + r, s, land_h[layer, 1, s, r])
                    cell_state[layer, 1 + r, :, cols] = land_c[layer, s, r]
            for side, there in from_sides:

                @pl.when(there)
                def _():
                    arrived(land_h.at[layer, 2 * side], r_h.at[layer, 2 * side])
                    arrived(land_cs.at[layer, side], r_cs.at[layer, side])
                    first = 0 if side == 0 else span - 2
                    for s in range(seqs):
                        cols = slice(s * width, (s + 1) * width)
                        for r in range(2):
                            put_taps(layer + 1, first + r, s, land_h[layer, 2 * side, s, r])
                        cell_state[layer, 0 if side == 0 else band + 1, :, cols] = land_cs[layer, side, s]

        @pl.when(layer == 0)
        def _():
            for s in range(seqs):
                for r in range(band):
                    put_taps(t_frame, 2 + r, s, frames[t, core * seqs + s, r])
            for side, there in from_sides:

                @pl.when(there)
                def _():
                    arrived(land_f.at[t, side], r_f.at[t, side])
                    first = 0 if side == 0 else span - 2
                    for s in range(seqs):
                        for r in range(2):
                            put_taps(t_frame, first + r, s, land_f[t, side, s, r])

        w_h = wbuf[layer, 7 * ch : 11 * ch, :]
        for r in range(1, band + 3):
            acc_h[r - 1] = jnp.dot(w_h, window(layer + 1, r), preferred_element_type=F32)

        for side, there in from_sides:

            @pl.when(there)
            def _():
                @pl.when(k > 0)
                def _():
                    arrived(m_land.at[prev, side], r_ml.at[prev, side])
                    for s in range(seqs):
                        put_taps(t_mem, 0 if side == 0 else span - 1, s, m_land[prev, side, s])

        w_m = wbuf[layer, 11 * ch : 14 * ch, :]
        for r in range(1, band + 3):
            acc_m[r - 1] = jnp.dot(w_m, window(t_mem, r), preferred_element_type=F32)

        for side, there in from_sides:

            @pl.when(there)
            def _():
                @pl.when(k > 0)
                def _():
                    arrived(h_land.at[prev, side], r_hl.at[prev, side])
                    first = 0 if side == 0 else span - 2
                    for s in range(seqs):
                        for r in range(2):
                            put_taps(before + 1, first + r, s, h_land[prev, side, s, r])

        w_x = wbuf[layer, : 7 * ch, :]
        for r in range(1, band + 3):
            a = jnp.dot(w_x, window(layer, r), preferred_element_type=F32)
            q = r - 1
            part = lambda n: a[n * ch : (n + 1) * ch]
            of_h = lambda n: acc_h[q, n * ch : (n + 1) * ch, :]
            of_m = lambda n: acc_m[q, n * ch : (n + 1) * ch, :]
            c_new = sig(part(1) + of_h(1) + 1.0) * cell_state[layer, q].astype(F32) + sig(
                part(0) + of_h(0)
            ) * jnp.tanh(part(2) + of_h(2))
            m_new = sig(part(4) + of_m(1) + 1.0) * mem_state[q].astype(F32) + sig(
                part(3) + of_m(0)
            ) * jnp.tanh(part(5) + of_m(2))
            if r == 1:
                c_new = jnp.where(has_up, c_new, 0.0)
                m_new = jnp.where(has_up, m_new, 0.0)
            if r == band + 2:
                c_new = jnp.where(has_down, c_new, 0.0)
                m_new = jnp.where(has_down, m_new, 0.0)
            c_new = c_new.astype(BF16)
            m_new = m_new.astype(BF16)
            cell_state[layer, q] = c_new
            mem_state[q] = m_new
            own = 2 <= r < band + 2
            for s in range(seqs):
                cols = slice(s * width, (s + 1) * width)
                put_taps(t_cell, r, s, c_new[:, cols])
                put_taps(t_mem, r, s, m_new[:, cols])
                if own:
                    cell_last[layer, s, r - 2] = c_new[:, cols]
                    m_send[k, s, r - 2] = m_new[:, cols]
            if own:
                acc_o[r - 2] = part(6) + of_h(3)

        for side, there in sides:

            @pl.when(there)
            def _():
                @pl.when(k < cells - 1)
                def _():
                    m_copy(k, side).start()

        w_c = wbuf[layer, 14 * ch : 16 * ch, :]
        w_n = wbuf[layer, 16 * ch : 18 * ch, :]
        for r in range(2, band + 2):
            both = jnp.dot(w_c, window(t_cell, r), preferred_element_type=F32)
            both = both + jnp.dot(w_n, window(t_mem, r), preferred_element_type=F32)
            h_new = (sig(acc_o[r - 2] + both[:ch]) * jnp.tanh(both[ch:])).astype(BF16)
            for s in range(seqs):
                h_send[k, s, r - 2] = h_new[:, s * width : (s + 1) * width]

        for side, there in sides:

            @pl.when(there)
            def _():
                @pl.when(k < cells - 1)
                def _():
                    h_copy(k, side).start()

        for s in range(seqs):
            for r in range(band):
                put_taps(layer + 1, 2 + r, s, h_send[k, s, r])
        return carry

    lax.fori_loop(0, cells, step, 0)

    last = cells - layers
    far_layers = pl.ds(last + other * local_layers, local_layers)
    own_layers = pl.ds(last + core * local_layers, local_layers)
    far_out = [
        remote(h_send.at[far_layers], hid_out.at[:, mine], s_out.at[0], r_out.at[0], other, row),
        remote(cell_last.at[pl.ds(other * local_layers, local_layers)], cell_out.at[:, mine],
               s_out.at[1], r_out.at[1], other, row),
        remote(m_send.at[last + other * local_layers + local_layers - 1], mem_out.at[0, mine],
               s_out.at[2], r_out.at[2], other, row),
    ]
    own_out = [
        pltpu.make_async_copy(h_send.at[own_layers], hid_out.at[:, mine], l_out.at[0]),
        pltpu.make_async_copy(cell_last.at[pl.ds(core * local_layers, local_layers)],
                              cell_out.at[:, mine], l_out.at[1]),
        pltpu.make_async_copy(m_send.at[last + core * local_layers + local_layers - 1],
                              mem_out.at[0, mine], l_out.at[2]),
    ]
    for copy in far_out + own_out:
        copy.start()

    for j in range(local_layers):
        for copy in center_copies(j)[1]:
            copy.wait_send()
    for side, there in sides:

        @pl.when(there)
        def _():
            memory_copy(side).wait_send()
            for t in range(steps):
                frame_copy(t, side).wait_send()
            for j in range(local_layers):
                for copy in halo_copies(j, side):
                    copy.wait_send()

            def drain(k, carry):
                h_copy(k, side).wait_send()
                m_copy(k, side).wait_send()
                return carry

            lax.fori_loop(0, cells - 1, drain, 0)

    for copy in own_out:
        copy.wait()
    for copy in far_out:
        copy.wait_send()
    arrived(hid_out.at[:, theirs], r_out.at[0])
    arrived(cell_out.at[:, theirs], r_out.at[1])
    arrived(mem_out.at[0, theirs], r_out.at[2])


def pack(w_x, w_h, w_m, w_o, w_last):
    layers, depth, _ = w_x.shape
    ch = w_last.shape[2]
    taps = depth // ch
    split = w_o.reshape(layers, taps, 2, ch, ch)
    mix = w_last.reshape(layers, 2, ch, ch)
    pieces = [w_x, w_h, w_m]
    for half in range(2):
        pieces.append(split[:, :, half].reshape(layers, depth, ch))
        middle = (taps // 2) * ch
        pieces.append(jnp.pad(mix[:, half], ((0, 0), (middle, depth - middle - ch), (0, 0))))
    return jnp.concatenate(pieces, axis=2).transpose(0, 2, 1)


def on_device(rows_total, cores, frames, hidden_in, cell_in, memory_in, w_x, w_h, w_m, w_o, w_last):
    steps = frames.shape[0]
    local_layers, seqs_all, band, ch, width = hidden_in.shape
    layers = local_layers * cores
    seqs = seqs_all // cores
    cells = layers * steps
    lanes = seqs * width
    weights = pack(w_x, w_h, w_m, w_o, w_last)
    block = (seqs, band, ch, width)
    dma = pltpu.SemaphoreType.DMA
    vm = lambda *shape: pltpu.VMEM(shape, BF16)
    vf = lambda *shape: pltpu.VMEM(shape, F32)
    in_vmem = pl.BlockSpec(memory_space=pltpu.VMEM)
    return pl.pallas_call(
        functools.partial(kernel, rows_total, layers, steps),
        out_shape=(
            jax.ShapeDtypeStruct(hidden_in.shape, BF16),
            jax.ShapeDtypeStruct(cell_in.shape, BF16),
            jax.ShapeDtypeStruct((1,) + memory_in.shape, BF16),
        ),
        in_specs=[in_vmem] * 4 + [pl.BlockSpec(memory_space=pl.ANY)],
        out_specs=(in_vmem,) * 3,
        scratch_shapes=[
            vm(layers + 3, (band + 4) * 3 * ch, lanes),
            vm(layers, *weights.shape[1:]),
            vm(layers, 3, *block),
            vm(layers, *block),
            vm(layers, 2, seqs, ch, width),
            vm(2, *block),
            vm(steps, 2, *block),
            vm(cells, *block),
            vm(cells, 2, *block),
            vm(cells, *block),
            vm(cells, 2, seqs, ch, width),
            vm(layers, band + 2, ch, lanes),
            vm(band + 2, ch, lanes),
            vm(layers, *block),
            vf(band + 2, 4 * ch, lanes),
            vf(band + 2, 3 * ch, lanes),
            vf(band, ch, lanes),
            dma((layers,)), dma((local_layers,)),
            dma((layers, 3)), dma((local_layers, cores, 2)), dma((local_layers,)),
            dma((layers,)), dma((layers, 2)), dma((local_layers, cores, 2)), dma((local_layers,)),
            dma((2,)), dma((2,)),
            dma((steps, 2)), dma((steps, 2)),
            dma((cells, 2)), dma((cells, 2)),
            dma((cells, 2)), dma((cells, 2)),
            dma((3,)), dma((3,)), dma((3,)),
        ],
        compiler_params=pltpu.CompilerParams(
            collective_id=0, has_side_effects=True, vmem_limit_bytes=48 * 1024 * 1024
        ),
    )(frames, hidden_in, cell_in, memory_in, weights)


def solution(mesh):
    return jax.shard_map(
        functools.partial(on_device, mesh.shape["rows"], mesh.shape["layer"]),
        mesh=mesh,
        in_specs=(
            P(None, None, "rows", None, None),
            P("layer", None, "rows", None, None),
            P("layer", None, "rows", None, None),
            P(None, "rows", None, None),
            P("layer", None, None),
            P("layer", None, None),
            P("layer", None, None),
            P("layer", None, None),
            P("layer", None, None),
        ),
        out_specs=(
            P("layer", None, "rows", None, None),
            P("layer", None, "rows", None, None),
            P("layer", None, "rows", None, None),
        ),
        check_vma=False,
    )
```

```python
import functools

import jax
import jax.numpy as jnp
from jax import lax
from jax.experimental import pallas as pl
from jax.experimental.pallas import tpu as pltpu
from jax.sharding import PartitionSpec as P

MESH = pl.DeviceIdType.MESH
F32 = jnp.float32
BF16 = jnp.bfloat16


def sig(x):
    return 0.5 * jnp.tanh(0.5 * x) + 0.5


def kernel(
    rows_total, layers, steps,
    frames, hidden, cell, memory, w_x, w_h, w_m, w_o, w_l,
    hid_out, cell_out, mem_out,
    taps, pair, b_x, b_h, b_m, b_o, b_l, land_h, land_c, land_cs, land_m, land_f,
    h_send, h_land, m_send, m_land, cell_state, mem_state, cell_last, acc_h, acc_m, acc_o,
    r_w, s_w, r_h, s_h, s_hc, r_c, r_cs, s_c, s_cc, r_m, s_m, r_f, s_f,
    r_hl, s_hl, r_ml, s_ml, r_out, s_out, l_out,
):
    core, row = lax.axis_index("layer"), lax.axis_index("rows")
    other = 1 - core
    local_layers, seqs_all, band, ch, width = hidden.shape
    cores = layers // local_layers
    seqs = seqs_all // cores
    cells = layers * steps
    tap = 3 * ch
    span = band + 4
    t_frame, t_mem = 0, layers + 1
    weights = ((w_x, b_x), (w_h, b_h), (w_m, b_m), (w_o, b_o), (w_l, b_l))
    has_up, has_down = row > 0, row < rows_total - 1
    up, down = lax.rem(row + rows_total - 1, rows_total), lax.rem(row + 1, rows_total)

    def to(c, r):
        return {"layer": c, "rows": r}

    def remote(src, dst, send, recv, c, r):
        return pltpu.make_async_remote_copy(
            src_ref=src, dst_ref=dst, send_sem=send, recv_sem=recv,
            device_id=to(c, r), device_id_type=MESH,
        )

    def arrived(dst, sem):
        pltpu.make_async_copy(dst, dst, sem).wait()

    lane = lax.broadcasted_iota(jnp.int32, (ch, width), 1)

    def shifts(value):
        wide = value.astype(F32)
        left = jnp.where(lane == 0, 0.0, pltpu.roll(wide, 1, 1)).astype(BF16)
        right = jnp.where(lane == width - 1, 0.0, pltpu.roll(wide, width - 1, 1)).astype(BF16)
        return left, value, right

    def put_pair(half, r, s, three):
        for b in range(3):
            start = (r - 1) * 2 * tap + (2 * b + half) * ch
            pair[start : start + ch, s * width : (s + 1) * width] = three[b]

    def put_taps(index, r, s, value, three=None):
        left, _, right = three or shifts(value)
        cols = slice(s * width, (s + 1) * width)
        taps[index, r * tap : r * tap + ch, cols] = left
        taps[index, r * tap + ch : r * tap + 2 * ch, cols] = value.astype(BF16)
        taps[index, r * tap + 2 * ch : (r + 1) * tap, cols] = right

    def window(index, r):
        return taps[index, (r - 1) * tap : (r + 2) * tap, :]

    barrier = pltpu.get_barrier_semaphore()
    pl.semaphore_signal(barrier, inc=1, device_id=to(other, row), device_id_type=MESH)

    @pl.when(has_up)
    def _():
        for c in range(cores):
            pl.semaphore_signal(barrier, inc=1, device_id=to(c, up), device_id_type=MESH)

    @pl.when(has_down)
    def _():
        for c in range(cores):
            pl.semaphore_signal(barrier, inc=1, device_id=to(c, down), device_id_type=MESH)

    edge = 2 * tap
    for index in range(layers + 2):
        taps[index, :edge, :] = jnp.zeros((edge, taps.shape[2]), BF16)
        taps[index, (span - 2) * tap :, :] = jnp.zeros((edge, taps.shape[2]), BF16)
    mem_state[0] = jnp.zeros(mem_state.shape[1:], BF16)
    mem_state[band + 1] = jnp.zeros(mem_state.shape[1:], BF16)
    for layer in range(layers):
        cell_state[layer, 0] = jnp.zeros(mem_state.shape[1:], BF16)
        cell_state[layer, band + 1] = jnp.zeros(mem_state.shape[1:], BF16)

    near = has_up.astype(jnp.int32) + has_down.astype(jnp.int32)
    pl.semaphore_wait(barrier, 1 + cores * near)

    mine = pl.ds(core * seqs, seqs)
    theirs = pl.ds(other * seqs, seqs)

    def center_copies(j):
        layer = core * local_layers + j
        local = [
            pltpu.make_async_copy(hidden.at[j, mine], land_h.at[layer, 1], r_h.at[layer, 1]),
            pltpu.make_async_copy(cell.at[j, mine], land_c.at[layer], r_c.at[layer]),
        ]
        far = [
            remote(hidden.at[j, theirs], land_h.at[layer, 1], s_hc.at[j], r_h.at[layer, 1], other, row),
            remote(cell.at[j, theirs], land_c.at[layer], s_cc.at[j], r_c.at[layer], other, row),
        ]
        for n, (w, b) in enumerate(weights):
            local.append(pltpu.make_async_copy(w.at[j], b.at[layer], r_w.at[layer, n]))
            far.append(remote(w.at[j], b.at[layer], s_w.at[j, n], r_w.at[layer, n], other, row))
        return local, far

    def halo_copies(j, side):
        layer = core * local_layers + j
        target = down if side == 0 else up
        edge_row = band - 1 if side == 0 else 0
        result = []
        for c in range(cores):
            part = pl.ds(c * seqs, seqs)
            result.append(remote(hidden.at[j, part], land_h.at[layer, 2 * side],
                                 s_h.at[j, c, side], r_h.at[layer, 2 * side], c, target))
            result.append(remote(cell.at[j, part, edge_row], land_cs.at[layer, side],
                                 s_c.at[j, c, side], r_cs.at[layer, side], c, target))
        return result

    def frame_copy(t, side):
        target = down if side == 0 else up
        return remote(frames.at[t, mine], land_f.at[t, side], s_f.at[t, side], r_f.at[t, side], core, target)

    def memory_copy(side):
        target = down if side == 0 else up
        return remote(memory.at[mine], land_m.at[side], s_m.at[side], r_m.at[side], core, target)

    sides = ((0, has_down), (1, has_up))
    from_sides = ((0, has_up), (1, has_down))

    for j in range(local_layers):
        local, far = center_copies(j)
        for copy in far + local:
            copy.start()
        for side, there in sides:

            @pl.when(there)
            def _():
                if j == 0:
                    memory_copy(side).start()
                    frame_copy(0, side).start()
                for copy in halo_copies(j, side):
                    copy.start()

    for t in range(1, steps):
        for side, there in sides:

            @pl.when(there)
            def _():
                frame_copy(t, side).start()

    for s in range(seqs):
        cols = slice(s * width, (s + 1) * width)
        for r in range(band):
            value = memory[core * seqs + s, r]
            put_taps(t_mem, 2 + r, s, value)
            mem_state[1 + r, :, cols] = value
    for side, there in from_sides:

        @pl.when(there)
        def _():
            arrived(land_m.at[side], r_m.at[side])
            first = 0 if side == 0 else span - 2
            for s in range(seqs):
                cols = slice(s * width, (s + 1) * width)
                for r in range(2):
                    put_taps(t_mem, first + r, s, land_m[side, s, r])
                if side == 0:
                    mem_state[0, :, cols] = land_m[side, s, band - 1]
                else:
                    mem_state[band + 1, :, cols] = land_m[side, s, 0]

    def h_copy(k, side):
        target = down if side == 0 else up
        return remote(h_send.at[k], h_land.at[k, side], s_hl.at[k, side], r_hl.at[k, side], core, target)

    def m_copy(k, side):
        target = down if side == 0 else up
        edge_row = 0 if side == 0 else band - 1
        return remote(m_send.at[k, :, edge_row], m_land.at[k, side], s_ml.at[k, side], r_ml.at[k, side], core, target)

    def step(k, carry):
        layer = lax.rem(k, layers)
        t = lax.div(k, layers)
        prev = lax.rem(k + cells - 1, cells)
        before = lax.rem(k + layers - 1, layers)

        @pl.when(k < layers)
        def _():
            for n, (_, b) in enumerate(weights):
                arrived(b.at[layer], r_w.at[layer, n])
            arrived(land_h.at[layer, 1], r_h.at[layer, 1])
            arrived(land_c.at[layer], r_c.at[layer])
            for s in range(seqs):
                cols = slice(s * width, (s + 1) * width)
                for r in range(band):
                    put_taps(layer + 1, 2 + r, s, land_h[layer, 1, s, r])
                    cell_state[layer, 1 + r, :, cols] = land_c[layer, s, r]
            for side, there in from_sides:

                @pl.when(there)
                def _():
                    arrived(land_h.at[layer, 2 * side], r_h.at[layer, 2 * side])
                    arrived(land_cs.at[layer, side], r_cs.at[layer, side])
                    first = 0 if side == 0 else span - 2
                    for s in range(seqs):
                        cols = slice(s * width, (s + 1) * width)
                        for r in range(2):
                            put_taps(layer + 1, first + r, s, land_h[layer, 2 * side, s, r])
                        cell_state[layer, 0 if side == 0 else band + 1, :, cols] = land_cs[layer, side, s]

        @pl.when(layer == 0)
        def _():
            for s in range(seqs):
                for r in range(band):
                    put_taps(t_frame, 2 + r, s, frames[t, core * seqs + s, r])
            for side, there in from_sides:

                @pl.when(there)
                def _():
                    arrived(land_f.at[t, side], r_f.at[t, side])
                    first = 0 if side == 0 else span - 2
                    for s in range(seqs):
                        for r in range(2):
                            put_taps(t_frame, first + r, s, land_f[t, side, s, r])

        h_w = b_h[layer]
        for r in range(1, band + 3):
            acc_h[r - 1] = jnp.dot(h_w, window(layer + 1, r), preferred_element_type=F32)

        for side, there in from_sides:

            @pl.when(there)
            def _():
                @pl.when(k > 0)
                def _():
                    arrived(m_land.at[prev, side], r_ml.at[prev, side])
                    for s in range(seqs):
                        put_taps(t_mem, 0 if side == 0 else span - 1, s, m_land[prev, side, s])

        m_w = b_m[layer]
        for r in range(1, band + 3):
            acc_m[r - 1] = jnp.dot(m_w, window(t_mem, r), preferred_element_type=F32)

        for side, there in from_sides:

            @pl.when(there)
            def _():
                @pl.when(k > 0)
                def _():
                    arrived(h_land.at[prev, side], r_hl.at[prev, side])
                    first = 0 if side == 0 else span - 2
                    for s in range(seqs):
                        for r in range(2):
                            put_taps(before + 1, first + r, s, h_land[prev, side, s, r])

        x_w = b_x[layer]
        for r in range(1, band + 3):
            a = jnp.dot(x_w, window(layer, r), preferred_element_type=F32)
            q = r - 1
            part = lambda n: a[n * ch : (n + 1) * ch]
            of_h = lambda n: acc_h[q, n * ch : (n + 1) * ch, :]
            of_m = lambda n: acc_m[q, n * ch : (n + 1) * ch, :]
            c_new = sig(part(1) + of_h(1) + 1.0) * cell_state[layer, q].astype(F32) + sig(
                part(0) + of_h(0)
            ) * jnp.tanh(part(2) + of_h(2))
            m_new = sig(part(4) + of_m(1) + 1.0) * mem_state[q].astype(F32) + sig(
                part(3) + of_m(0)
            ) * jnp.tanh(part(5) + of_m(2))
            if r == 1:
                c_new = jnp.where(has_up, c_new, 0.0)
                m_new = jnp.where(has_up, m_new, 0.0)
            if r == band + 2:
                c_new = jnp.where(has_down, c_new, 0.0)
                m_new = jnp.where(has_down, m_new, 0.0)
            c_new = c_new.astype(BF16)
            m_new = m_new.astype(BF16)
            cell_state[layer, q] = c_new
            mem_state[q] = m_new
            own = 2 <= r < band + 2
            for s in range(seqs):
                cols = slice(s * width, (s + 1) * width)
                three = shifts(m_new[:, cols])
                put_pair(0, r, s, shifts(c_new[:, cols]))
                put_pair(1, r, s, three)
                put_taps(t_mem, r, s, m_new[:, cols], three)
                if own:
                    cell_last[layer, s, r - 2] = c_new[:, cols]
                    m_send[k, s, r - 2] = m_new[:, cols]
            if own:
                acc_o[r - 2] = part(6) + of_h(3)

        for side, there in sides:

            @pl.when(there)
            def _():
                @pl.when(k < cells - 1)
                def _():
                    m_copy(k, side).start()

        o_w = b_o[layer]
        l_w = b_l[layer]
        for r in range(2, band + 2):
            start = (r - 2) * 2 * tap
            middle = start + 2 * tap + 2 * ch
            gate = jnp.dot(o_w, pair[start : start + 6 * tap, :], preferred_element_type=F32)
            mixed = jnp.dot(l_w, pair[middle : middle + 2 * ch, :], preferred_element_type=F32)
            h_new = (sig(acc_o[r - 2] + gate) * jnp.tanh(mixed)).astype(BF16)
            for s in range(seqs):
                h_send[k, s, r - 2] = h_new[:, s * width : (s + 1) * width]

        for side, there in sides:

            @pl.when(there)
            def _():
                @pl.when(k < cells - 1)
                def _():
                    h_copy(k, side).start()

        for s in range(seqs):
            for r in range(band):
                put_taps(layer + 1, 2 + r, s, h_send[k, s, r])
        return carry

    lax.fori_loop(0, cells, step, 0)

    last = cells - layers
    far_layers = pl.ds(last + other * local_layers, local_layers)
    own_layers = pl.ds(last + core * local_layers, local_layers)
    far_out = [
        remote(h_send.at[far_layers], hid_out.at[:, mine], s_out.at[0], r_out.at[0], other, row),
        remote(cell_last.at[pl.ds(other * local_layers, local_layers)], cell_out.at[:, mine],
               s_out.at[1], r_out.at[1], other, row),
        remote(m_send.at[last + other * local_layers + local_layers - 1], mem_out.at[0, mine],
               s_out.at[2], r_out.at[2], other, row),
    ]
    own_out = [
        pltpu.make_async_copy(h_send.at[own_layers], hid_out.at[:, mine], l_out.at[0]),
        pltpu.make_async_copy(cell_last.at[pl.ds(core * local_layers, local_layers)],
                              cell_out.at[:, mine], l_out.at[1]),
        pltpu.make_async_copy(m_send.at[last + core * local_layers + local_layers - 1],
                              mem_out.at[0, mine], l_out.at[2]),
    ]
    for copy in far_out + own_out:
        copy.start()

    for j in range(local_layers):
        for copy in center_copies(j)[1]:
            copy.wait_send()
    for side, there in sides:

        @pl.when(there)
        def _():
            memory_copy(side).wait_send()
            for t in range(steps):
                frame_copy(t, side).wait_send()
            for j in range(local_layers):
                for copy in halo_copies(j, side):
                    copy.wait_send()

            def drain(k, carry):
                h_copy(k, side).wait_send()
                m_copy(k, side).wait_send()
                return carry

            lax.fori_loop(0, cells - 1, drain, 0)

    for copy in own_out:
        copy.wait()
    for copy in far_out:
        copy.wait_send()
    arrived(hid_out.at[:, theirs], r_out.at[0])
    arrived(cell_out.at[:, theirs], r_out.at[1])
    arrived(mem_out.at[0, theirs], r_out.at[2])


def on_device(rows_total, cores, frames, hidden_in, cell_in, memory_in, w_x, w_h, w_m, w_o, w_last):
    steps = frames.shape[0]
    local_layers, seqs_all, band, ch, width = hidden_in.shape
    layers = local_layers * cores
    seqs = seqs_all // cores
    cells = layers * steps
    lanes = seqs * width
    weights = [w.transpose(0, 2, 1) for w in (w_x, w_h, w_m, w_o, w_last)]
    block = (seqs, band, ch, width)
    dma = pltpu.SemaphoreType.DMA
    vm = lambda *shape: pltpu.VMEM(shape, BF16)
    vf = lambda *shape: pltpu.VMEM(shape, F32)
    in_vmem = pl.BlockSpec(memory_space=pltpu.VMEM)
    return pl.pallas_call(
        functools.partial(kernel, rows_total, layers, steps),
        out_shape=(
            jax.ShapeDtypeStruct(hidden_in.shape, BF16),
            jax.ShapeDtypeStruct(cell_in.shape, BF16),
            jax.ShapeDtypeStruct((1,) + memory_in.shape, BF16),
        ),
        in_specs=[in_vmem] * 4 + [pl.BlockSpec(memory_space=pl.ANY)] * len(weights),
        out_specs=(in_vmem,) * 3,
        scratch_shapes=[
            vm(layers + 2, (band + 4) * 3 * ch, lanes),
            vm((band + 2) * 6 * ch, lanes),
            *[vm(layers, *w.shape[1:]) for w in weights],
            vm(layers, 3, *block),
            vm(layers, *block),
            vm(layers, 2, seqs, ch, width),
            vm(2, *block),
            vm(steps, 2, *block),
            vm(cells, *block),
            vm(cells, 2, *block),
            vm(cells, *block),
            vm(cells, 2, seqs, ch, width),
            vm(layers, band + 2, ch, lanes),
            vm(band + 2, ch, lanes),
            vm(layers, *block),
            vf(band + 2, 4 * ch, lanes),
            vf(band + 2, 3 * ch, lanes),
            vf(band, ch, lanes),
            dma((layers, len(weights))), dma((local_layers, len(weights))),
            dma((layers, 3)), dma((local_layers, cores, 2)), dma((local_layers,)),
            dma((layers,)), dma((layers, 2)), dma((local_layers, cores, 2)), dma((local_layers,)),
            dma((2,)), dma((2,)),
            dma((steps, 2)), dma((steps, 2)),
            dma((cells, 2)), dma((cells, 2)),
            dma((cells, 2)), dma((cells, 2)),
            dma((3,)), dma((3,)), dma((3,)),
        ],
        compiler_params=pltpu.CompilerParams(
            collective_id=0, has_side_effects=True, vmem_limit_bytes=48 * 1024 * 1024
        ),
    )(frames, hidden_in, cell_in, memory_in, *weights)


def solution(mesh):
    return jax.shard_map(
        functools.partial(on_device, mesh.shape["rows"], mesh.shape["layer"]),
        mesh=mesh,
        in_specs=(
            P(None, None, "rows", None, None),
            P("layer", None, "rows", None, None),
            P("layer", None, "rows", None, None),
            P(None, "rows", None, None),
            P("layer", None, None),
            P("layer", None, None),
            P("layer", None, None),
            P("layer", None, None),
            P("layer", None, None),
        ),
        out_specs=(
            P("layer", None, "rows", None, None),
            P("layer", None, "rows", None, None),
            P("layer", None, "rows", None, None),
        ),
        check_vma=False,
    )
```

```python
import functools

import jax
import jax.numpy as jnp
from jax import lax
from jax.experimental import pallas as pl
from jax.experimental.pallas import tpu as pltpu
from jax.sharding import PartitionSpec as P

MESH = pl.DeviceIdType.MESH
F32 = jnp.float32
BF16 = jnp.bfloat16


def sig(x):
    return 0.5 * jnp.tanh(0.5 * x) + 0.5


def kernel(
    rows_total, layers, steps,
    frames, hidden, cell, memory, w_x, w_h, w_m, w_o, w_l,
    hid_out, cell_out, mem_out,
    taps, pair, b_x, b_h, b_m, b_o, b_l, land_h, land_c, land_cs, land_m, land_f, m_in, f_in,
    h_send, h_land, m_send, m_land, cell_state, mem_state, cell_last, acc_h, acc_m, acc_o,
    r_w, s_w, r_h, s_h, s_hc, r_c, r_cs, s_c, s_cc, r_m, s_m, r_f, s_f, l_m, l_f,
    r_hl, s_hl, r_ml, s_ml, r_out, s_out, l_out,
):
    core, row = lax.axis_index("layer"), lax.axis_index("rows")
    other = 1 - core
    local_layers, seqs_all, band, ch, width = hidden.shape
    cores = layers // local_layers
    seqs = seqs_all // cores
    cells = layers * steps
    tap = 3 * ch
    span = band + 4
    t_frame, t_mem = 0, layers + 1
    weights = ((w_x, b_x), (w_h, b_h), (w_m, b_m), (w_o, b_o), (w_l, b_l))
    has_up, has_down = row > 0, row < rows_total - 1
    up, down = lax.rem(row + rows_total - 1, rows_total), lax.rem(row + 1, rows_total)

    def to(c, r):
        return {"layer": c, "rows": r}

    def remote(src, dst, send, recv, c, r):
        return pltpu.make_async_remote_copy(
            src_ref=src, dst_ref=dst, send_sem=send, recv_sem=recv,
            device_id=to(c, r), device_id_type=MESH,
        )

    def arrived(dst, sem):
        pltpu.make_async_copy(dst, dst, sem).wait()

    lane = lax.broadcasted_iota(jnp.int32, (ch, width), 1)

    def shifts(value):
        wide = value.astype(F32)
        left = jnp.where(lane == 0, 0.0, pltpu.roll(wide, 1, 1)).astype(BF16)
        right = jnp.where(lane == width - 1, 0.0, pltpu.roll(wide, width - 1, 1)).astype(BF16)
        return left, value, right

    def put_pair(half, r, s, three):
        for b in range(3):
            start = (r - 1) * 2 * tap + (2 * b + half) * ch
            pair[start : start + ch, s * width : (s + 1) * width] = three[b]

    def put_taps(index, r, s, value, three=None):
        left, _, right = three or shifts(value)
        cols = slice(s * width, (s + 1) * width)
        taps[index, r * tap : r * tap + ch, cols] = left
        taps[index, r * tap + ch : r * tap + 2 * ch, cols] = value.astype(BF16)
        taps[index, r * tap + 2 * ch : (r + 1) * tap, cols] = right

    def window(index, r):
        return taps[index, (r - 1) * tap : (r + 2) * tap, :]

    barrier = pltpu.get_barrier_semaphore()
    pl.semaphore_signal(barrier, inc=1, device_id=to(other, row), device_id_type=MESH)

    @pl.when(has_up)
    def _():
        for c in range(cores):
            pl.semaphore_signal(barrier, inc=1, device_id=to(c, up), device_id_type=MESH)

    @pl.when(has_down)
    def _():
        for c in range(cores):
            pl.semaphore_signal(barrier, inc=1, device_id=to(c, down), device_id_type=MESH)

    edge = 2 * tap
    for index in range(layers + 2):
        taps[index, :edge, :] = jnp.zeros((edge, taps.shape[2]), BF16)
        taps[index, (span - 2) * tap :, :] = jnp.zeros((edge, taps.shape[2]), BF16)
    mem_state[0] = jnp.zeros(mem_state.shape[1:], BF16)
    mem_state[band + 1] = jnp.zeros(mem_state.shape[1:], BF16)
    for layer in range(layers):
        cell_state[layer, 0] = jnp.zeros(mem_state.shape[1:], BF16)
        cell_state[layer, band + 1] = jnp.zeros(mem_state.shape[1:], BF16)

    near = has_up.astype(jnp.int32) + has_down.astype(jnp.int32)
    pl.semaphore_wait(barrier, 1 + cores * near)

    mine = pl.ds(core * seqs, seqs)
    theirs = pl.ds(other * seqs, seqs)

    def center_copies(j):
        layer = core * local_layers + j
        local = [
            pltpu.make_async_copy(hidden.at[j, mine], land_h.at[layer, 1], r_h.at[layer, 1]),
            pltpu.make_async_copy(cell.at[j, mine], land_c.at[layer], r_c.at[layer]),
        ]
        far = [
            remote(hidden.at[j, theirs], land_h.at[layer, 1], s_hc.at[j], r_h.at[layer, 1], other, row),
            remote(cell.at[j, theirs], land_c.at[layer], s_cc.at[j], r_c.at[layer], other, row),
        ]
        for n, (w, b) in enumerate(weights):
            local.append(pltpu.make_async_copy(w.at[j], b.at[layer], r_w.at[layer, n]))
            far.append(remote(w.at[j], b.at[layer], s_w.at[j, n], r_w.at[layer, n], other, row))
        return local, far

    def halo_copies(j, side):
        layer = core * local_layers + j
        target = down if side == 0 else up
        edge_row = band - 1 if side == 0 else 0
        result = []
        for c in range(cores):
            part = pl.ds(c * seqs, seqs)
            result.append(remote(hidden.at[j, part], land_h.at[layer, 2 * side],
                                 s_h.at[j, c, side], r_h.at[layer, 2 * side], c, target))
            result.append(remote(cell.at[j, part, edge_row], land_cs.at[layer, side],
                                 s_c.at[j, c, side], r_cs.at[layer, side], c, target))
        return result

    def frame_copy(t, side):
        target = down if side == 0 else up
        return remote(frames.at[t, mine], land_f.at[t, side], s_f.at[t, side], r_f.at[t, side], core, target)

    def memory_copy(side):
        target = down if side == 0 else up
        return remote(memory.at[mine], land_m.at[side], s_m.at[side], r_m.at[side], core, target)

    sides = ((0, has_down), (1, has_up))
    from_sides = ((0, has_up), (1, has_down))

    own_memory = pltpu.make_async_copy(memory.at[mine], m_in, l_m.at[0])
    own_memory.start()
    own_frames = [pltpu.make_async_copy(frames.at[t, mine], f_in.at[t], l_f.at[t]) for t in range(steps)]
    for copy in own_frames:
        copy.start()

    for j in range(local_layers):
        local, far = center_copies(j)
        for copy in far + local:
            copy.start()
        for side, there in sides:

            @pl.when(there)
            def _():
                if j == 0:
                    memory_copy(side).start()
                    frame_copy(0, side).start()
                for copy in halo_copies(j, side):
                    copy.start()

    for t in range(1, steps):
        for side, there in sides:

            @pl.when(there)
            def _():
                frame_copy(t, side).start()

    for copy in [own_memory] + own_frames:
        copy.wait()
    for s in range(seqs):
        cols = slice(s * width, (s + 1) * width)
        for r in range(band):
            value = m_in[s, r]
            put_taps(t_mem, 2 + r, s, value)
            mem_state[1 + r, :, cols] = value
    for side, there in from_sides:

        @pl.when(there)
        def _():
            arrived(land_m.at[side], r_m.at[side])
            first = 0 if side == 0 else span - 2
            for s in range(seqs):
                cols = slice(s * width, (s + 1) * width)
                for r in range(2):
                    put_taps(t_mem, first + r, s, land_m[side, s, r])
                if side == 0:
                    mem_state[0, :, cols] = land_m[side, s, band - 1]
                else:
                    mem_state[band + 1, :, cols] = land_m[side, s, 0]

    def h_copy(k, side):
        target = down if side == 0 else up
        return remote(h_send.at[k], h_land.at[k, side], s_hl.at[k, side], r_hl.at[k, side], core, target)

    def m_copy(k, side):
        target = down if side == 0 else up
        edge_row = 0 if side == 0 else band - 1
        return remote(m_send.at[k, :, edge_row], m_land.at[k, side], s_ml.at[k, side], r_ml.at[k, side], core, target)

    def step(k, carry):
        layer = lax.rem(k, layers)
        t = lax.div(k, layers)
        prev = lax.rem(k + cells - 1, cells)
        before = lax.rem(k + layers - 1, layers)

        @pl.when(k < layers)
        def _():
            for n, (_, b) in enumerate(weights):
                arrived(b.at[layer], r_w.at[layer, n])
            arrived(land_h.at[layer, 1], r_h.at[layer, 1])
            arrived(land_c.at[layer], r_c.at[layer])
            for s in range(seqs):
                cols = slice(s * width, (s + 1) * width)
                for r in range(band):
                    put_taps(layer + 1, 2 + r, s, land_h[layer, 1, s, r])
                    cell_state[layer, 1 + r, :, cols] = land_c[layer, s, r]
            for side, there in from_sides:

                @pl.when(there)
                def _():
                    arrived(land_h.at[layer, 2 * side], r_h.at[layer, 2 * side])
                    arrived(land_cs.at[layer, side], r_cs.at[layer, side])
                    first = 0 if side == 0 else span - 2
                    for s in range(seqs):
                        cols = slice(s * width, (s + 1) * width)
                        for r in range(2):
                            put_taps(layer + 1, first + r, s, land_h[layer, 2 * side, s, r])
                        cell_state[layer, 0 if side == 0 else band + 1, :, cols] = land_cs[layer, side, s]

        @pl.when(layer == 0)
        def _():
            for s in range(seqs):
                for r in range(band):
                    put_taps(t_frame, 2 + r, s, f_in[t, s, r])
            for side, there in from_sides:

                @pl.when(there)
                def _():
                    arrived(land_f.at[t, side], r_f.at[t, side])
                    first = 0 if side == 0 else span - 2
                    for s in range(seqs):
                        for r in range(2):
                            put_taps(t_frame, first + r, s, land_f[t, side, s, r])

        h_w = b_h[layer]
        for r in range(1, band + 3):
            acc_h[r - 1] = jnp.dot(h_w, window(layer + 1, r), preferred_element_type=F32)

        for side, there in from_sides:

            @pl.when(there)
            def _():
                @pl.when(k > 0)
                def _():
                    arrived(m_land.at[prev, side], r_ml.at[prev, side])
                    for s in range(seqs):
                        put_taps(t_mem, 0 if side == 0 else span - 1, s, m_land[prev, side, s])

        m_w = b_m[layer]
        for r in range(1, band + 3):
            acc_m[r - 1] = jnp.dot(m_w, window(t_mem, r), preferred_element_type=F32)

        def take_rows(side, there):
            @pl.when(there)
            def _():
                @pl.when(k > 0)
                def _():
                    arrived(h_land.at[prev, side], r_hl.at[prev, side])
                    first = 0 if side == 0 else span - 2
                    for s in range(seqs):
                        for r in range(2):
                            put_taps(before + 1, first + r, s, h_land[prev, side, s, r])

        x_w = b_x[layer]
        for r in range(1, band + 3):
            if r == 1:
                take_rows(0, has_up)
            if r == band + 1:
                take_rows(1, has_down)
            a = jnp.dot(x_w, window(layer, r), preferred_element_type=F32)
            q = r - 1
            part = lambda n: a[n * ch : (n + 1) * ch]
            of_h = lambda n: acc_h[q, n * ch : (n + 1) * ch, :]
            of_m = lambda n: acc_m[q, n * ch : (n + 1) * ch, :]
            c_new = sig(part(1) + of_h(1) + 1.0) * cell_state[layer, q].astype(F32) + sig(
                part(0) + of_h(0)
            ) * jnp.tanh(part(2) + of_h(2))
            m_new = sig(part(4) + of_m(1) + 1.0) * mem_state[q].astype(F32) + sig(
                part(3) + of_m(0)
            ) * jnp.tanh(part(5) + of_m(2))
            if r == 1:
                c_new = jnp.where(has_up, c_new, 0.0)
                m_new = jnp.where(has_up, m_new, 0.0)
            if r == band + 2:
                c_new = jnp.where(has_down, c_new, 0.0)
                m_new = jnp.where(has_down, m_new, 0.0)
            c_new = c_new.astype(BF16)
            m_new = m_new.astype(BF16)
            cell_state[layer, q] = c_new
            mem_state[q] = m_new
            own = 2 <= r < band + 2
            for s in range(seqs):
                cols = slice(s * width, (s + 1) * width)
                three = shifts(m_new[:, cols])
                put_pair(0, r, s, shifts(c_new[:, cols]))
                put_pair(1, r, s, three)
                put_taps(t_mem, r, s, m_new[:, cols], three)
                if own:
                    cell_last[layer, s, r - 2] = c_new[:, cols]
                    m_send[k, s, r - 2] = m_new[:, cols]
            if own:
                acc_o[r - 2] = part(6) + of_h(3)

        for side, there in sides:

            @pl.when(there)
            def _():
                @pl.when(k < cells - 1)
                def _():
                    m_copy(k, side).start()

        o_w = b_o[layer]
        l_w = b_l[layer]
        for r in range(2, band + 2):
            start = (r - 2) * 2 * tap
            middle = start + 2 * tap + 2 * ch
            gate = jnp.dot(o_w, pair[start : start + 6 * tap, :], preferred_element_type=F32)
            mixed = jnp.dot(l_w, pair[middle : middle + 2 * ch, :], preferred_element_type=F32)
            h_new = (sig(acc_o[r - 2] + gate) * jnp.tanh(mixed)).astype(BF16)
            for s in range(seqs):
                h_send[k, s, r - 2] = h_new[:, s * width : (s + 1) * width]

        for side, there in sides:

            @pl.when(there)
            def _():
                @pl.when(k < cells - 1)
                def _():
                    h_copy(k, side).start()

        for s in range(seqs):
            for r in range(band):
                put_taps(layer + 1, 2 + r, s, h_send[k, s, r])
        return carry

    lax.fori_loop(0, cells, step, 0)

    last = cells - layers
    far_layers = pl.ds(last + other * local_layers, local_layers)
    own_layers = pl.ds(last + core * local_layers, local_layers)
    far_out = [
        remote(h_send.at[far_layers], hid_out.at[:, mine], s_out.at[0], r_out.at[0], other, row),
        remote(cell_last.at[pl.ds(other * local_layers, local_layers)], cell_out.at[:, mine],
               s_out.at[1], r_out.at[1], other, row),
        remote(m_send.at[last + other * local_layers + local_layers - 1], mem_out.at[0, mine],
               s_out.at[2], r_out.at[2], other, row),
    ]
    own_out = [
        pltpu.make_async_copy(h_send.at[own_layers], hid_out.at[:, mine], l_out.at[0]),
        pltpu.make_async_copy(cell_last.at[pl.ds(core * local_layers, local_layers)],
                              cell_out.at[:, mine], l_out.at[1]),
        pltpu.make_async_copy(m_send.at[last + core * local_layers + local_layers - 1],
                              mem_out.at[0, mine], l_out.at[2]),
    ]
    for copy in far_out + own_out:
        copy.start()

    for j in range(local_layers):
        for copy in center_copies(j)[1]:
            copy.wait_send()
    for side, there in sides:

        @pl.when(there)
        def _():
            memory_copy(side).wait_send()
            for t in range(steps):
                frame_copy(t, side).wait_send()
            for j in range(local_layers):
                for copy in halo_copies(j, side):
                    copy.wait_send()

            def drain(k, carry):
                h_copy(k, side).wait_send()
                m_copy(k, side).wait_send()
                return carry

            lax.fori_loop(0, cells - 1, drain, 0)

    for copy in own_out:
        copy.wait()
    for copy in far_out:
        copy.wait_send()
    arrived(hid_out.at[:, theirs], r_out.at[0])
    arrived(cell_out.at[:, theirs], r_out.at[1])
    arrived(mem_out.at[0, theirs], r_out.at[2])


def on_device(rows_total, cores, frames, hidden_in, cell_in, memory_in, w_x, w_h, w_m, w_o, w_last):
    steps = frames.shape[0]
    local_layers, seqs_all, band, ch, width = hidden_in.shape
    layers = local_layers * cores
    seqs = seqs_all // cores
    cells = layers * steps
    lanes = seqs * width
    weights = [w.transpose(0, 2, 1) for w in (w_x, w_h, w_m, w_o, w_last)]
    block = (seqs, band, ch, width)
    dma = pltpu.SemaphoreType.DMA
    vm = lambda *shape: pltpu.VMEM(shape, BF16)
    vf = lambda *shape: pltpu.VMEM(shape, F32)
    in_vmem = pl.BlockSpec(memory_space=pltpu.VMEM)
    return pl.pallas_call(
        functools.partial(kernel, rows_total, layers, steps),
        out_shape=(
            jax.ShapeDtypeStruct(hidden_in.shape, BF16),
            jax.ShapeDtypeStruct(cell_in.shape, BF16),
            jax.ShapeDtypeStruct((1,) + memory_in.shape, BF16),
        ),
        in_specs=[pl.BlockSpec(memory_space=pl.ANY)] * (4 + len(weights)),
        out_specs=(in_vmem,) * 3,
        scratch_shapes=[
            vm(layers + 2, (band + 4) * 3 * ch, lanes),
            vm((band + 2) * 6 * ch, lanes),
            *[vm(layers, *w.shape[1:]) for w in weights],
            vm(layers, 3, *block),
            vm(layers, *block),
            vm(layers, 2, seqs, ch, width),
            vm(2, *block),
            vm(steps, 2, *block),
            vm(*block),
            vm(steps, *block),
            vm(cells, *block),
            vm(cells, 2, *block),
            vm(cells, *block),
            vm(cells, 2, seqs, ch, width),
            vm(layers, band + 2, ch, lanes),
            vm(band + 2, ch, lanes),
            vm(layers, *block),
            vf(band + 2, 4 * ch, lanes),
            vf(band + 2, 3 * ch, lanes),
            vf(band, ch, lanes),
            dma((layers, len(weights))), dma((local_layers, len(weights))),
            dma((layers, 3)), dma((local_layers, cores, 2)), dma((local_layers,)),
            dma((layers,)), dma((layers, 2)), dma((local_layers, cores, 2)), dma((local_layers,)),
            dma((2,)), dma((2,)),
            dma((steps, 2)), dma((steps, 2)), dma((1,)), dma((steps,)),
            dma((cells, 2)), dma((cells, 2)),
            dma((cells, 2)), dma((cells, 2)),
            dma((3,)), dma((3,)), dma((3,)),
        ],
        compiler_params=pltpu.CompilerParams(
            collective_id=0, has_side_effects=True, vmem_limit_bytes=62 * 1024 * 1024
        ),
    )(frames, hidden_in, cell_in, memory_in, *weights)


def solution(mesh):
    return jax.shard_map(
        functools.partial(on_device, mesh.shape["rows"], mesh.shape["layer"]),
        mesh=mesh,
        in_specs=(
            P(None, None, "rows", None, None),
            P("layer", None, "rows", None, None),
            P("layer", None, "rows", None, None),
            P(None, "rows", None, None),
            P("layer", None, None),
            P("layer", None, None),
            P("layer", None, None),
            P("layer", None, None),
            P("layer", None, None),
        ),
        out_specs=(
            P("layer", None, "rows", None, None),
            P("layer", None, "rows", None, None),
            P("layer", None, "rows", None, None),
        ),
        check_vma=False,
    )
```
